32 devices in a mesh: curve: 16 (over z, y, core), chan: 2 (over x).
Axes of the slice: x: 2, y: 2, z: 4, core: 2. Of those that a mesh axis runs over, the one named last changes fastest.
Arguments:
- features: bfloat16 [65536, 256], P('curve', 'chan'), may hold values from -6 to 6
- cotangent: bfloat16 [65536, 256], P('curve', 'chan'), may hold values from -6 to 6
- near_kernel: bfloat16 [512, 8, 128, 128], P('curve'), may hold values from -0.1875 to 0.1875
- near_index: int32 [512, 8], P('curve'), may hold values from 0 to 511, as said below
- near_count: int32 [512], P('curve'), may hold values from 1 to 8, as said below
- basis_in: bfloat16 [512, 16, 128], P('curve'), may hold values from -0.09375 to 0.09375
- basis_out: bfloat16 [512, 128, 16], P('curve'), may hold values from -1.5 to 1.5
- far_kernel: float32 [16, 8, 16, 16], P('curve'), may hold values from -0.5 to 0.5
- far_index: int32 [16, 8], P('curve'), may hold values from 0 to 15, as said below
- channel_mix: float32 [256, 256], replicated, may hold values from -0.375 to 0.375
Outputs:
- layer_out: bfloat16 [65536, 256], P('curve', 'chan')
- feature_grad: bfloat16 [65536, 256], P('curve', 'chan')
The draws below stay inside these ranges and needn't reach their ends.
Inputs may be any that keep to these rules, and one draw needn't show every extreme that they name: `near_index`: slot 0 of block b holds b; every slot of block b holds a block from b - 32 to b. `near_count`: in every group of 32 blocks one block has all 8 slots live and another block has one. `far_index`: every partner of group g differs from g by 2 or more.
All inputs are finite; a program needn't handle non-finite values.
Results may differ from the reference program's by a relative error of at most 0.006.
Values may be sent and summed in bfloat16 or wider, within the bound.
A program may use at most 128 MiB of HBM per device.

```python
import jax
import jax.numpy as jnp
from jax import lax

P_SIZE = 128
C = 256
R = 16
S = 8
A = 8
NB_DEV = 32
G = 16
NB = 512
PANELS = 65536


def draw_near_index(key, part):
    block_ids = jnp.arange(NB, dtype=jnp.int32)
    back_steps = jax.random.randint(key, (NB, S), 0, NB_DEV + 1)
    chosen = jnp.maximum(block_ids[:, None] - back_steps, 0)
    slot_ids = jnp.arange(S, dtype=jnp.int32)
    return jnp.where(slot_ids[None, :] == 0, block_ids[:, None], chosen).astype(jnp.int32)


def draw_near_count(key, part):
    key_group = jax.random.fold_in(key, 11)
    key_block = jax.random.fold_in(key, 23)
    key_full = jax.random.fold_in(key, 37)
    key_single = jax.random.fold_in(key, 41)
    ceiling = jax.random.randint(key_group, (G,), 2, S + 1)
    per_block = jnp.repeat(ceiling, NB_DEV)
    raw_count = jax.random.randint(key_block, (NB,), 1, per_block + 1)
    full_pos = jax.random.randint(key_full, (G,), 0, NB_DEV)
    offset = jax.random.randint(key_single, (G,), 1, NB_DEV)
    single_pos = (full_pos + offset) % NB_DEV
    full_rep = jnp.repeat(full_pos, NB_DEV)
    single_rep = jnp.repeat(single_pos, NB_DEV)
    position = jnp.arange(NB, dtype=jnp.int32) % NB_DEV
    shaped = jnp.where(position == single_rep, 1, raw_count)
    return jnp.where(position == full_rep, S, shaped).astype(jnp.int32)


def draw_far_index(key, part):
    offsets = jax.random.randint(key, (G, A), 2, G - 1)
    group_ids = jnp.arange(G, dtype=jnp.int32)[:, None]
    partners = (group_ids + offsets) % G
    slot_ids = jnp.arange(A, dtype=jnp.int32)[None, :]
    partners = jnp.where((group_ids == 0) & (slot_ids == 0), G - 1, partners)
    partners = jnp.where((group_ids == G - 1) & (slot_ids == 0), 0, partners)
    return partners.astype(jnp.int32)


def block_levels(own_key, shape, shards, low, high):
    gain = 1.0
    for dim, parts in shards:
        draws = jax.random.uniform(jax.random.fold_in(jax.random.fold_in(own_key, 6), dim), (parts,), jnp.float32, low / len(shards), high / len(shards))
        gain = gain * jnp.repeat(jnp.exp(draws), shape[dim] // parts).reshape((-1,) + (1,) * (len(shape) - 1 - dim))
    return gain


def bell_draw(key, dims, scale, limit, pieces=(), kind=jnp.bfloat16):
    array = scale * jax.random.normal(key, dims, jnp.float32)
    if pieces:
        array = array * block_levels(key, dims, pieces, -0.22, 0.18)
    return jnp.clip(array, -limit, limit).astype(kind)


def setup_inputs(seed: int = 0) -> dict:
    arg_keys = jax.random.split(jax.random.key(seed), 11)
    return {
        "features": bell_draw(arg_keys[0], (PANELS, C), 1.0, 6.0, ((0, 16), (1, 2))),
        "cotangent": bell_draw(arg_keys[1], (PANELS, C), 1.0, 6.0, ((0, 16), (1, 2))),
        "near_kernel": bell_draw(arg_keys[2], (NB, S, P_SIZE, P_SIZE), (P_SIZE * S) ** -0.5, 0.1875, ((0, 16),)),
        "near_index": draw_near_index(jax.random.fold_in(arg_keys[10], 71), 0),
        "near_count": draw_near_count(jax.random.fold_in(arg_keys[10], 71), 0),
        "basis_in": bell_draw(arg_keys[5], (NB, R, P_SIZE), (P_SIZE * NB_DEV) ** -0.5, 0.09375, ((0, 16),)),
        "basis_out": bell_draw(arg_keys[6], (NB, P_SIZE, R), R ** -0.5, 1.5, ((0, 16),)),
        "far_kernel": bell_draw(arg_keys[7], (G, A, R, R), (R * A) ** -0.5, 0.5, ((0, 16),), jnp.float32),
        "far_index": draw_far_index(jax.random.fold_in(arg_keys[10], 71), 0),
        "channel_mix": bell_draw(arg_keys[9], (C, C), C ** -0.5, 0.375, (), jnp.float32),
    }


def reference(features, cotangent, near_kernel, near_index, near_count, basis_in, basis_out, far_kernel, far_index, channel_mix):
    exact = lax.Precision.HIGHEST
    feat_blocks = features.reshape(NB, P_SIZE, C)
    cot_blocks = cotangent.reshape(NB, P_SIZE, C)
    live_slot = (jnp.arange(S, dtype=jnp.int32)[None, :] < near_count[:, None]).astype(jnp.float32)

    def group_coef(group):
        first_row = (group * NB_DEV).astype(jnp.int32)
        basis_src = lax.dynamic_slice_in_dim(basis_in, first_row, NB_DEV, 0).astype(jnp.float32)
        basis_dst = lax.dynamic_slice_in_dim(basis_out, first_row, NB_DEV, 0).astype(jnp.float32)
        feat_here = lax.dynamic_slice_in_dim(feat_blocks, first_row, NB_DEV, 0).astype(jnp.float32)
        cot_here = lax.dynamic_slice_in_dim(cot_blocks, first_row, NB_DEV, 0).astype(jnp.float32)
        coef = jnp.einsum('brp,bpc->rc', basis_src, feat_here)
        back = jnp.einsum('bpr,bpc->rc', basis_dst, cot_here)
        return coef, back

    coef_all, dfar = lax.map(group_coef, jnp.arange(G, dtype=jnp.int32))
    coarse = coef_all.astype(jnp.bfloat16)
    mixed = jnp.einsum('grc,ck->grk', coarse.astype(jnp.float32), channel_mix, precision=exact)
    far_coef = jnp.einsum('gaqr,garc->gqc', far_kernel, mixed[far_index], precision=exact).astype(jnp.bfloat16)
    spread = jnp.einsum('gaqr,gqc->garc', far_kernel, dfar, precision=exact)
    dmixed = jax.ops.segment_sum(spread.reshape(G * A, R, C), far_index.reshape(G * A), num_segments=G)
    dcoarse = jnp.einsum('grk,ck->grc', dmixed, channel_mix, precision=exact).astype(jnp.bfloat16)

    def group_near(group):
        first_row = (group * NB_DEV).astype(jnp.int32)
        tiles = lax.dynamic_slice_in_dim(near_kernel, first_row, NB_DEV, 0).astype(jnp.float32)
        slot_rows = lax.dynamic_slice_in_dim(near_index, first_row, NB_DEV, 0)
        slot_live = lax.dynamic_slice_in_dim(live_slot, first_row, NB_DEV, 0)
        picked = feat_blocks[slot_rows].astype(jnp.float32) * slot_live[:, :, None, None]
        near = jnp.einsum('bspq,bsqc->bpc', tiles, picked)
        basis_dst = lax.dynamic_slice_in_dim(basis_out, first_row, NB_DEV, 0).astype(jnp.float32)
        far_here = lax.dynamic_index_in_dim(far_coef, group, 0, keepdims=False).astype(jnp.float32)
        layer = near + jnp.einsum('bpr,rc->bpc', basis_dst, far_here)
        cot_here = lax.dynamic_slice_in_dim(cot_blocks, first_row, NB_DEV, 0).astype(jnp.float32)
        contrib = jnp.einsum('bspq,bpc->bsqc', tiles, cot_here) * slot_live[:, :, None, None]
        local_rows = slot_rows - (first_row - NB_DEV)
        one_hot = (local_rows[:, :, None] == jnp.arange(2 * NB_DEV, dtype=jnp.int32)[None, None, :]).astype(jnp.float32)
        extended = jnp.einsum('bse,bsqc->eqc', one_hot, contrib)
        return layer.astype(jnp.bfloat16), extended

    layer_all, extended = lax.map(group_near, jnp.arange(G, dtype=jnp.int32))
    own_part = extended[:, NB_DEV:]
    left_part = extended[:, :NB_DEV]
    moved = jnp.concatenate([left_part[1:], jnp.zeros_like(left_part[:1])], axis=0)
    nearback = (own_part + moved).reshape(NB, P_SIZE, C)
    dcoarse_rep = jnp.repeat(dcoarse, NB_DEV, axis=0).astype(jnp.float32)
    grad = nearback + jnp.einsum('brp,brc->bpc', basis_in.astype(jnp.float32), dcoarse_rep)
    return layer_all.reshape(PANELS, C), grad.astype(jnp.bfloat16).reshape(PANELS, C)
```

```python
import functools

import jax
import jax.numpy as jnp
from jax import lax
from jax.experimental import pallas as pl
from jax.experimental.pallas import tpu as pltpu
from jax.sharding import PartitionSpec as P

F32 = jnp.float32
BF16 = jnp.bfloat16
EXACT = lax.Precision.HIGHEST
VMEM_LIMIT = 40 * 1024 * 1024
STEP = 4


def shifted(value, axis, steps):
    count = lax.axis_size(axis)
    leading, last = (max(0, -steps), min(count, count - steps))
    return lax.ppermute(value, axis, [(source, source + steps) for source in range(leading, last)])


def cover(shape):
    zeros = (0,) * len(shape)
    return pl.BlockSpec(shape, lambda *_: zeros)


def params():
    return pltpu.CompilerParams(vmem_limit_bytes=VMEM_LIMIT)


def bundle_kernel(chan_ref, x_ref, dy_ref, bin_ref, bout_ref, far_ref, part_ref, out_ref):
    blocks, rank, width = bin_ref.shape[0], bin_ref.shape[1], x_ref.shape[2]
    coarse = jnp.zeros((rank, width), F32)
    dfar = jnp.zeros((rank, width), F32)
    for b in range(blocks):
        coarse += jnp.dot(bin_ref[b], x_ref[b], preferred_element_type=F32)
        dfar += lax.dot_general(
            bout_ref[b], dy_ref[b], (((0,), (0,)), ((), ())), preferred_element_type=F32
        )
    out_ref[0:rank] = coarse.astype(BF16)
    out_ref[rank : 2 * rank] = dfar.astype(BF16)
    far = far_ref[...]
    high = far.astype(BF16).astype(F32)
    low = far - high
    out_ref[2 * rank : 3 * rank] = jnp.where(chan_ref[0] == 0, high, low).astype(BF16)
    out_ref[3 * rank : 4 * rank] = jnp.broadcast_to(part_ref[...], (rank, width)).astype(BF16)


def far_kernel_body(rank, place_ref, part_ref, every_ref, far_ref, mix_ref, far_out, back_out):
    group, chan = place_ref[0], place_ref[1]
    shares = mix_ref.shape[0] // far_out.shape[1]
    width = far_out.shape[1]
    groups = every_ref.shape[0] // shares
    partners = far_ref.shape[1] // rank
    cols = pl.ds(pl.multiple_of(chan * width, width), width)
    far = far_ref[...]
    high = far.astype(BF16)
    low = (far - high.astype(F32)).astype(BF16)
    picked = jnp.concatenate(
        [
            jnp.concatenate(
                [every_ref[part_ref[a] * shares + s, 0:rank] for a in range(partners)], axis=0
            )
            for s in range(shares)
        ],
        axis=1,
    )
    coef = jnp.dot(high, picked, preferred_element_type=F32) + jnp.dot(
        low, picked, preferred_element_type=F32
    )
    far_out[...] = jnp.dot(
        coef, mix_ref[:, cols], precision=EXACT, preferred_element_type=F32
    ).astype(BF16)
    total = jnp.zeros((partners * rank, shares * width), F32)
    span = min(groups, 16)
    for first in range(0, groups, span):
        grads = jnp.concatenate(
            [
                jnp.concatenate(
                    [
                        every_ref[g * shares + s, rank : 2 * rank]
                        for g in range(first, first + span)
                    ],
                    axis=0,
                )
                for s in range(shares)
            ],
            axis=1,
        )
        for s in range(2):
            mats = []
            for g in range(first, first + span):
                here = every_ref[g * shares + s, 3 * rank : 4 * rank].astype(F32) == group.astype(F32)
                mats.append(
                    jnp.where(here, every_ref[g * shares + s, 2 * rank : 3 * rank].astype(F32), 0.0)
                )
            chosen = jnp.concatenate(mats, axis=0).astype(BF16)
            total += lax.dot_general(
                chosen, grads, (((0,), (0,)), ((), ())), preferred_element_type=F32
            )
    dmixed = total[0:rank]
    for a in range(1, partners):
        dmixed += total[a * rank : (a + 1) * rank]
    back_out[...] = lax.dot_general(
        dmixed,
        mix_ref[cols, :],
        (((1,), (1,)), ((), ())),
        precision=EXACT,
        preferred_element_type=F32,
    ).astype(BF16)


def backward_kernel(target_ref, tile_ref, dy_ref, left_ref, own_ref, total):
    step = pl.program_id(0)
    blocks = left_ref.shape[0]
    slots, panels = tile_ref.shape[1], tile_ref.shape[2]

    @pl.when(step == 0)
    def _():
        @pl.loop(0, 2 * blocks)
        def _(row):
            total[row] = jnp.zeros(total.shape[1:], F32)

    for i in range(STEP):
        turned = dy_ref[i].T
        first = (step * STEP + i) * slots
        for k in range(0, slots, 2):
            pair = jnp.concatenate([tile_ref[i, k], tile_ref[i, k + 1]], axis=1)
            term = jnp.dot(turned, pair, preferred_element_type=F32)
            total[target_ref[first + k]] += term[:, :panels]
            total[target_ref[first + k + 1]] += term[:, panels:]

    @pl.when(step == pl.num_programs(0) - 1)
    def _():
        @pl.loop(0, blocks)
        def _(row):
            left_ref[row] = total[row].astype(BF16)
            own_ref[row] = total[blocks + row]


def forward_kernel(source_ref, tile_ref, before_ref, x_ref, bout_ref, far_ref, out_ref, held):
    step = pl.program_id(0)
    blocks = x_ref.shape[0]
    slots = tile_ref.shape[1]

    @pl.when(step == 0)
    def _():
        @pl.loop(0, blocks)
        def _(row):
            held[row] = before_ref[row]
            held[blocks + row] = x_ref[row]

        held[2 * blocks] = jnp.zeros(held.shape[1:], BF16)

    far = far_ref[...]
    for i in range(STEP):
        first = (step * STEP + i) * slots
        tiles = jnp.concatenate([tile_ref[i, k] for k in range(slots)], axis=1)
        rows = jnp.concatenate([held[source_ref[first + k]] for k in range(slots)], axis=0)
        near = jnp.dot(tiles, rows, preferred_element_type=F32)
        near += jnp.dot(bout_ref[i], far, preferred_element_type=F32)
        out_ref[i] = near.astype(BF16)


def gradient_kernel(own_ref, arrived_ref, bin_ref, back_ref, out_ref):
    back = back_ref[...]
    for i in range(own_ref.shape[0]):
        turned = own_ref[i] + arrived_ref[i].astype(F32)
        term = lax.dot_general(
            back, bin_ref[i], (((0,), (0,)), ((), ())), preferred_element_type=F32
        )
        out_ref[i] = (turned + term).T.astype(BF16)


def body(
    features,
    cotangent,
    near_kernel,
    near_index,
    near_count,
    basis_in,
    basis_out,
    far_kernel,
    far_index,
    channel_mix,
):
    blocks, slots, panels, _ = near_kernel.shape
    width = features.shape[1]
    rank = basis_in.shape[1]
    partners = far_index.shape[1]
    position = lax.axis_index("curve")
    chan_pos = lax.axis_index("chan")
    x = features.reshape(blocks, panels, width)
    dy = cotangent.reshape(blocks, panels, width)
    before = shifted(features, "curve", 1).reshape(blocks, panels, width)
    live_slot = lax.iota(jnp.int32, slots)[None, :] < near_count[:, None]
    rows = near_index - (position * blocks - blocks)
    rows = jnp.where(live_slot, rows, 2 * blocks).reshape(-1)
    far_flat = far_kernel[0].transpose(1, 0, 2).reshape(rank, partners * rank)
    part_row = jnp.repeat(far_index[0], rank)[None, :].astype(F32)
    tile_shape = (panels, width)
    steps = (blocks // STEP,)

    def by_step(*shape):
        zeros = (0,) * (len(shape) - 1)
        return pl.BlockSpec(shape, lambda n, *_: (n,) + zeros)

    own_bundle = pl.pallas_call(
        bundle_kernel,
        out_shape=jax.ShapeDtypeStruct((4 * rank, width), BF16),
        in_specs=[pl.BlockSpec(memory_space=pltpu.SMEM)]
        + [pl.BlockSpec(memory_space=pltpu.VMEM)] * 6,
        out_specs=pl.BlockSpec(memory_space=pltpu.VMEM),
        compiler_params=params(),
        name="bundle",
    )(chan_pos[None], x, dy, basis_in, basis_out, far_flat, part_row)
    every = lax.all_gather(own_bundle, ("curve", "chan"), axis=0)

    half_flops = 2 * blocks * slots * panels * panels * width
    tile_bytes = 2 * near_kernel.size
    left, own = pl.pallas_call(
        backward_kernel,
        out_shape=(
            jax.ShapeDtypeStruct((blocks, width, panels), BF16),
            jax.ShapeDtypeStruct((blocks, width, panels), F32),
        ),
        grid_spec=pltpu.PrefetchScalarGridSpec(
            num_scalar_prefetch=1,
            grid=steps,
            in_specs=[by_step(STEP, slots, panels, panels), by_step(STEP, *tile_shape)],
            out_specs=(cover((blocks, width, panels)), cover((blocks, width, panels))),
            scratch_shapes=[pltpu.VMEM((2 * blocks + 1, width, panels), F32)],
        ),
        compiler_params=params(),
        cost_estimate=pl.CostEstimate(
            flops=4 * half_flops, bytes_accessed=2 * tile_bytes, transcendentals=0
        ),
        name="backward",
    )(rows, near_kernel, dy)
    arrived = shifted(left, "curve", -1)

    place = jnp.stack([position, chan_pos]).astype(jnp.int32)
    far_low, back_low = pl.pallas_call(
        functools.partial(far_kernel_body, rank),
        out_shape=(
            jax.ShapeDtypeStruct((rank, width), BF16),
            jax.ShapeDtypeStruct((rank, width), BF16),
        ),
        in_specs=[pl.BlockSpec(memory_space=pltpu.SMEM)] * 2
        + [pl.BlockSpec(memory_space=pltpu.VMEM)] * 3,
        out_specs=(pl.BlockSpec(memory_space=pltpu.VMEM),) * 2,
        compiler_params=params(),
        name="far",
    )(place, far_index[0], every, far_flat, channel_mix)

    layer = pl.pallas_call(
        forward_kernel,
        out_shape=jax.ShapeDtypeStruct((blocks, panels, width), BF16),
        grid_spec=pltpu.PrefetchScalarGridSpec(
            num_scalar_prefetch=1,
            grid=steps,
            in_specs=[
                by_step(STEP, slots, panels, panels),
                cover((blocks, panels, width)),
                cover((blocks, panels, width)),
                by_step(STEP, panels, rank),
                cover((rank, width)),
            ],
            out_specs=by_step(STEP, *tile_shape),
            scratch_shapes=[pltpu.VMEM((2 * blocks + 1, panels, width), BF16)],
        ),
        compiler_params=params(),
        cost_estimate=pl.CostEstimate(
            flops=4 * half_flops, bytes_accessed=2 * tile_bytes, transcendentals=0
        ),
        name="forward",
    )(rows, near_kernel, before, x, basis_out, far_low)

    grad = pl.pallas_call(
        gradient_kernel,
        out_shape=jax.ShapeDtypeStruct((blocks, panels, width), BF16),
        grid=steps,
        in_specs=[
            by_step(STEP, width, panels),
            by_step(STEP, width, panels),
            by_step(STEP, rank, panels),
            cover((rank, width)),
        ],
        out_specs=by_step(STEP, *tile_shape),
        compiler_params=params(),
        name="gradient",
    )(own, arrived, basis_in, back_low)
    return (layer.reshape(blocks * panels, width), grad.reshape(blocks * panels, width))


def solution(mesh):
    return jax.shard_map(
        body,
        mesh=mesh,
        in_specs=(
            P("curve", "chan"),
            P("curve", "chan"),
            P("curve", None, None, None),
            P("curve", None),
            P("curve"),
            P("curve", None, None),
            P("curve", None, None),
            P("curve", None, None, None),
            P("curve", None),
            P(),
        ),
        out_specs=(P("curve", "chan"), P("curve", "chan")),
        check_vma=False,
    )
```

```python
import functools

import jax
import jax.numpy as jnp
from jax import lax
from jax.experimental import pallas as pl
from jax.experimental.pallas import tpu as pltpu
from jax.sharding import PartitionSpec as P

F32 = jnp.float32
BF16 = jnp.bfloat16
EXACT = lax.Precision.HIGHEST
VMEM_LIMIT = 60 * 1024 * 1024
STEP = 4


def shifted(value, axis, steps):
    count = lax.axis_size(axis)
    leading, last = (max(0, -steps), min(count, count - steps))
    return lax.ppermute(value, axis, [(source, source + steps) for source in range(leading, last)])


def cover(shape):
    zeros = (0,) * len(shape)
    return pl.BlockSpec(shape, lambda *_: zeros)


def params(mib=60):
    return pltpu.CompilerParams(vmem_limit_bytes=mib * 1024 * 1024)


def bundle_kernel(part_ref, x_ref, dy_ref, bin_ref, bout_ref, far_ref, out_ref):
    blocks, rank, width = bin_ref.shape[0], bin_ref.shape[1], x_ref.shape[2]
    partners = far_ref.shape[0]
    coarse = jnp.zeros((rank, width), F32)
    dfar = jnp.zeros((rank, width), F32)
    for b in range(blocks):
        coarse += jnp.dot(bin_ref[b], x_ref[b], preferred_element_type=F32)
        dfar += lax.dot_general(
            bout_ref[b], dy_ref[b], (((0,), (0,)), ((), ())), preferred_element_type=F32
        )
    coarse = coarse.astype(BF16)
    spread = [
        lax.dot_general(
            far_ref[a], dfar, (((0,), (0,)), ((), ())), precision=EXACT, preferred_element_type=F32
        )
        for a in range(partners)
    ]

    @pl.loop(0, out_ref.shape[0])
    def _(group):
        share = jnp.zeros((rank, width), F32)
        for a in range(partners):
            share += jnp.where(part_ref[a] == group, 1.0, 0.0) * spread[a]
        out_ref[group, 0:rank] = coarse
        out_ref[group, rank : 2 * rank] = share.astype(BF16)


def exchange_kernel(
    groups, shares, part_ref, send_ref, far_ref, mix_ref, far_out, back_out,
    held, halves, joined, send_sem, recv_sem, send_half, recv_half,
):
    me, chan = lax.axis_index("curve"), lax.axis_index("chan")
    rank, width = far_out.shape
    partners = far_ref.shape[0]
    barrier = pltpu.get_barrier_semaphore()

    @pl.loop(1, groups)
    def _(step):
        pl.semaphore_signal(
            barrier,
            inc=1,
            device_id=(lax.rem(me + step, groups), chan),
            device_id_type=pl.DeviceIdType.MESH,
        )

    for step in range(1, shares):
        pl.semaphore_signal(
            barrier,
            inc=1,
            device_id=(me, lax.rem(chan + step, shares)),
            device_id_type=pl.DeviceIdType.MESH,
        )
    pl.semaphore_wait(barrier, groups + shares - 2)

    def along_curve(step):
        other = lax.rem(me + step, groups)
        return pltpu.make_async_remote_copy(
            src_ref=send_ref.at[other],
            dst_ref=held.at[me],
            send_sem=send_sem.at[step],
            recv_sem=recv_sem.at[step],
            device_id=(other, chan),
            device_id_type=pl.DeviceIdType.MESH,
        )

    @pl.loop(1, groups)
    def _(step):
        along_curve(step).start()

    held[me] = send_ref[me]

    @pl.loop(1, groups)
    def _(step):
        along_curve(step).wait()

    coef = jnp.zeros((rank, width), F32)
    for a in range(partners):
        far = far_ref[a]
        high = far.astype(BF16)
        low = (far - high.astype(F32)).astype(BF16)
        row = held[part_ref[a], 0:rank]
        coef += jnp.dot(high, row, preferred_element_type=F32)
        coef += jnp.dot(low, row, preferred_element_type=F32)
    total = lax.fori_loop(
        0,
        groups,
        lambda g, acc: acc + held[g, rank : 2 * rank].astype(F32),
        jnp.zeros((rank, width), F32),
    )
    own = pl.ds(pl.multiple_of(chan * width, width), width)
    for s in range(shares):
        part = slice(s * width, (s + 1) * width)
        halves[s, 0:rank] = jnp.dot(
            coef, mix_ref[own, part], precision=EXACT, preferred_element_type=F32
        )
        halves[s, rank : 2 * rank] = lax.dot_general(
            total,
            mix_ref[part, own],
            (((1,), (1,)), ((), ())),
            precision=EXACT,
            preferred_element_type=F32,
        )

    copies = []
    for step in range(1, shares):
        other = lax.rem(chan + step, shares)
        copies.append(
            pltpu.make_async_remote_copy(
                src_ref=halves.at[other],
                dst_ref=joined.at[step - 1],
                send_sem=send_half.at[step],
                recv_sem=recv_half.at[step],
                device_id=(me, other),
                device_id_type=pl.DeviceIdType.MESH,
            )
        )
        copies[-1].start()
    both = halves[chan]
    for step, copy in enumerate(copies):
        copy.wait()
        both += joined[step]
    far_out[...] = both[0:rank].astype(BF16)
    back_out[...] = both[rank : 2 * rank].astype(BF16)


def backward_kernel(target_ref, tile_ref, dy_ref, left_ref, own_ref, total):
    step = pl.program_id(0)
    blocks = left_ref.shape[0]
    slots, panels = tile_ref.shape[1], tile_ref.shape[2]

    @pl.when(step == 0)
    def _():
        @pl.loop(0, 2 * blocks + 1)
        def _(row):
            total[row] = jnp.zeros(total.shape[1:], F32)

    for i in range(STEP):
        turned = dy_ref[i].T
        first = (step * STEP + i) * slots
        for k in range(0, slots, 2):
            pair = jnp.concatenate([tile_ref[i, k], tile_ref[i, k + 1]], axis=1)
            term = jnp.dot(turned, pair, preferred_element_type=F32)
            total[target_ref[first + k]] += term[:, :panels]
            total[target_ref[first + k + 1]] += term[:, panels:]

    @pl.when(step == pl.num_programs(0) - 1)
    def _():
        @pl.loop(0, blocks)
        def _(row):
            left_ref[row] = total[row].astype(BF16)
            own_ref[row] = total[blocks + row]


def forward_kernel(source_ref, tile_ref, before_ref, x_ref, bout_ref, far_ref, out_ref, held):
    step = pl.program_id(0)
    blocks = x_ref.shape[0]
    slots = tile_ref.shape[1]

    @pl.when(step == 0)
    def _():
        @pl.loop(0, blocks)
        def _(row):
            held[row] = before_ref[row]
            held[blocks + row] = x_ref[row]

        held[2 * blocks] = jnp.zeros(held.shape[1:], BF16)

    far = far_ref[...]
    for i in range(STEP):
        first = (step * STEP + i) * slots
        tiles = jnp.concatenate([tile_ref[i, k] for k in range(slots)], axis=1)
        rows = jnp.concatenate([held[source_ref[first + k]] for k in range(slots)], axis=0)
        near = jnp.dot(tiles, rows, preferred_element_type=F32)
        near += jnp.dot(bout_ref[i], far, preferred_element_type=F32)
        out_ref[i] = near.astype(BF16)


def gradient_kernel(own_ref, arrived_ref, bin_ref, back_ref, out_ref):
    back = back_ref[...]
    panels = bin_ref.shape[2]
    row = lax.broadcasted_iota(jnp.int32, (panels, panels), 0)
    col = lax.broadcasted_iota(jnp.int32, (panels, panels), 1)
    eye = jnp.where(row == col, 1.0, 0.0).astype(BF16)
    twice = jnp.concatenate([eye, eye], axis=1)
    for i in range(own_ref.shape[0]):
        turned = own_ref[i] + arrived_ref[i].astype(F32)
        high = turned.astype(BF16)
        low = (turned - high.astype(F32)).astype(BF16)
        grad = lax.dot_general(
            twice,
            jnp.concatenate([high, low], axis=1),
            (((1,), (1,)), ((), ())),
            preferred_element_type=F32,
        )
        grad += lax.dot_general(
            bin_ref[i], back, (((0,), (0,)), ((), ())), preferred_element_type=F32
        )
        out_ref[i] = grad.astype(BF16)


def body(
    features,
    cotangent,
    near_kernel,
    near_index,
    near_count,
    basis_in,
    basis_out,
    far_kernel,
    far_index,
    channel_mix,
):
    blocks, slots, panels, _ = near_kernel.shape
    width = features.shape[1]
    rank = basis_in.shape[1]
    position = lax.axis_index("curve")
    x = features.reshape(blocks, panels, width)
    dy = cotangent.reshape(blocks, panels, width)
    before = shifted(features, "curve", 1).reshape(blocks, panels, width)
    live_slot = lax.iota(jnp.int32, slots)[None, :] < near_count[:, None]
    rows = near_index - (position * blocks - blocks)
    rows = jnp.where(live_slot, rows, 2 * blocks).reshape(-1)
    tile_shape = (panels, width)
    steps = (blocks // STEP,)

    def by_step(*shape):
        zeros = (0,) * (len(shape) - 1)
        return pl.BlockSpec(shape, lambda n, *_: (n,) + zeros)

    smem = pl.BlockSpec(memory_space=pltpu.SMEM)
    vmem = pl.BlockSpec(memory_space=pltpu.VMEM)
    groups, shares = lax.axis_size("curve"), lax.axis_size("chan")
    outgoing = pl.pallas_call(
        bundle_kernel,
        out_shape=jax.ShapeDtypeStruct((groups, 2 * rank, width), BF16),
        in_specs=[smem] + [vmem] * 5,
        out_specs=vmem,
        compiler_params=params(),
        name="bundle",
    )(far_index[0], x, dy, basis_in, basis_out, far_kernel[0])

    half_flops = 2 * blocks * slots * panels * panels * width
    tile_bytes = 2 * near_kernel.size
    left, own = pl.pallas_call(
        backward_kernel,
        out_shape=(
            jax.ShapeDtypeStruct((blocks, width, panels), BF16),
            jax.ShapeDtypeStruct((blocks, width, panels), F32),
        ),
        grid_spec=pltpu.PrefetchScalarGridSpec(
            num_scalar_prefetch=1,
            grid=steps,
            in_specs=[by_step(STEP, slots, panels, panels), by_step(STEP, *tile_shape)],
            out_specs=(cover((blocks, width, panels)), cover((blocks, width, panels))),
            scratch_shapes=[pltpu.VMEM((2 * blocks + 1, width, panels), F32)],
        ),
        compiler_params=params(),
        cost_estimate=pl.CostEstimate(
            flops=4 * half_flops, bytes_accessed=2 * tile_bytes, transcendentals=0
        ),
        name="backward",
    )(rows, near_kernel, dy)
    arrived = shifted(left, "curve", -1)

    far_low, back_low = pl.pallas_call(
        functools.partial(exchange_kernel, groups, shares),
        out_shape=(jax.ShapeDtypeStruct((rank, width), BF16),) * 2,
        in_specs=[smem] + [vmem] * 3,
        out_specs=(vmem, vmem),
        scratch_shapes=[
            pltpu.VMEM((groups, 2 * rank, width), BF16),
            pltpu.VMEM((shares, 2 * rank, width), F32),
            pltpu.VMEM((max(1, shares - 1), 2 * rank, width), F32),
            pltpu.SemaphoreType.DMA((groups,)),
            pltpu.SemaphoreType.DMA((groups,)),
            pltpu.SemaphoreType.DMA((shares,)),
            pltpu.SemaphoreType.DMA((shares,)),
        ],
        compiler_params=pltpu.CompilerParams(
            collective_id=0, has_side_effects=True, vmem_limit_bytes=VMEM_LIMIT
        ),
        name="exchange",
    )(far_index[0], outgoing, far_kernel[0], channel_mix)

    layer = pl.pallas_call(
        forward_kernel,
        out_shape=jax.ShapeDtypeStruct((blocks, panels, width), BF16),
        grid_spec=pltpu.PrefetchScalarGridSpec(
            num_scalar_prefetch=1,
            grid=steps,
            in_specs=[
                by_step(STEP, slots, panels, panels),
                cover((blocks, panels, width)),
                cover((blocks, panels, width)),
                by_step(STEP, panels, rank),
                cover((rank, width)),
            ],
            out_specs=by_step(STEP, *tile_shape),
            scratch_shapes=[pltpu.VMEM((2 * blocks + 1, panels, width), BF16)],
        ),
        compiler_params=params(58),
        cost_estimate=pl.CostEstimate(
            flops=4 * half_flops, bytes_accessed=2 * tile_bytes, transcendentals=0
        ),
        name="forward",
    )(rows, near_kernel, before, x, basis_out, far_low)

    grad = pl.pallas_call(
        gradient_kernel,
        out_shape=jax.ShapeDtypeStruct((blocks, panels, width), BF16),
        grid=steps,
        in_specs=[
            by_step(STEP, width, panels),
            by_step(STEP, width, panels),
            by_step(STEP, rank, panels),
            cover((rank, width)),
        ],
        out_specs=by_step(STEP, *tile_shape),
        compiler_params=params(52),
        name="gradient",
    )(own, arrived, basis_in, back_low)
    return (layer.reshape(blocks * panels, width), grad.reshape(blocks * panels, width))


def solution(mesh):
    return jax.shard_map(
        body,
        mesh=mesh,
        in_specs=(
            P("curve", "chan"),
            P("curve", "chan"),
            P("curve", None, None, None),
            P("curve", None),
            P("curve"),
            P("curve", None, None),
            P("curve", None, None),
            P("curve", None, None, None),
            P("curve", None),
            P(),
        ),
        out_specs=(P("curve", "chan"), P("curve", "chan")),
        check_vma=False,
    )
```

```python
import functools

import jax
import jax.numpy as jnp
from jax import lax
from jax.experimental import pallas as pl
from jax.experimental.pallas import tpu as pltpu
from jax.sharding import PartitionSpec as P

F32 = jnp.float32
BF16 = jnp.bfloat16
EXACT = lax.Precision.HIGHEST
STEP = 4


def shifted(value, axis, steps):
    count = lax.axis_size(axis)
    leading, last = (max(0, -steps), min(count, count - steps))
    return lax.ppermute(value, axis, [(source, source + steps) for source in range(leading, last)])


def cover(shape):
    zeros = (0,) * len(shape)
    return pl.BlockSpec(shape, lambda *_: zeros)


def params(mib=60):
    return pltpu.CompilerParams(vmem_limit_bytes=mib * 1024 * 1024)


def bundle_kernel(part_ref, x_ref, dy_ref, bin_ref, bout_ref, far_ref, out_ref):
    blocks, rank, width = bin_ref.shape[0], bin_ref.shape[1], x_ref.shape[2]
    partners = far_ref.shape[0]
    coarse = jnp.zeros((rank, width), F32)
    dfar = jnp.zeros((rank, width), F32)
    for b in range(blocks):
        coarse += jnp.dot(bin_ref[b], x_ref[b], preferred_element_type=F32)
        dfar += jnp.dot(bout_ref[b], dy_ref[b], preferred_element_type=F32)
    coarse = coarse.astype(BF16)
    spread = [
        lax.dot_general(
            far_ref[a], dfar, (((0,), (0,)), ((), ())), precision=EXACT, preferred_element_type=F32
        )
        for a in range(partners)
    ]

    @pl.loop(0, out_ref.shape[0])
    def _(group):
        share = jnp.zeros((rank, width), F32)
        for a in range(partners):
            share += jnp.where(part_ref[a] == group, 1.0, 0.0) * spread[a]
        out_ref[group, 0:rank] = coarse
        out_ref[group, rank : 2 * rank] = share.astype(BF16)


def exchange_kernel(
    groups, shares, part_ref, send_ref, far_ref, mix_ref, far_out, back_out,
    held, halves, joined, send_sem, recv_sem, send_half, recv_half,
):
    me, chan = lax.axis_index("curve"), lax.axis_index("chan")
    rank, width = far_out.shape
    partners = far_ref.shape[0]
    barrier = pltpu.get_barrier_semaphore()

    @pl.loop(1, groups)
    def _(step):
        pl.semaphore_signal(
            barrier,
            inc=1,
            device_id=(lax.rem(me + step, groups), chan),
            device_id_type=pl.DeviceIdType.MESH,
        )

    for step in range(1, shares):
        pl.semaphore_signal(
            barrier,
            inc=1,
            device_id=(me, lax.rem(chan + step, shares)),
            device_id_type=pl.DeviceIdType.MESH,
        )
    pl.semaphore_wait(barrier, groups + shares - 2)

    def along_curve(step):
        other = lax.rem(me + step, groups)
        return pltpu.make_async_remote_copy(
            src_ref=send_ref.at[other],
            dst_ref=held.at[me],
            send_sem=send_sem.at[step],
            recv_sem=recv_sem.at[step],
            device_id=(other, chan),
            device_id_type=pl.DeviceIdType.MESH,
        )

    @pl.loop(1, groups)
    def _(step):
        along_curve(step).start()

    held[me] = send_ref[me]

    @pl.loop(1, groups)
    def _(step):
        along_curve(step).wait()

    coef = jnp.zeros((rank, width), F32)
    for a in range(partners):
        far = far_ref[a]
        high = far.astype(BF16)
        low = (far - high.astype(F32)).astype(BF16)
        row = held[part_ref[a], 0:rank]
        coef += jnp.dot(high, row, preferred_element_type=F32)
        coef += jnp.dot(low, row, preferred_element_type=F32)
    total = lax.fori_loop(
        0,
        groups,
        lambda g, acc: acc + held[g, rank : 2 * rank].astype(F32),
        jnp.zeros((rank, width), F32),
    )
    own = pl.ds(pl.multiple_of(chan * width, width), width)
    for s in range(shares):
        part = slice(s * width, (s + 1) * width)
        halves[s, 0:rank] = jnp.dot(
            coef, mix_ref[own, part], precision=EXACT, preferred_element_type=F32
        )
        halves[s, rank : 2 * rank] = lax.dot_general(
            total,
            mix_ref[part, own],
            (((1,), (1,)), ((), ())),
            precision=EXACT,
            preferred_element_type=F32,
        )

    copies = []
    for step in range(1, shares):
        other = lax.rem(chan + step, shares)
        copies.append(
            pltpu.make_async_remote_copy(
                src_ref=halves.at[other],
                dst_ref=joined.at[step - 1],
                send_sem=send_half.at[step],
                recv_sem=recv_half.at[step],
                device_id=(me, other),
                device_id_type=pl.DeviceIdType.MESH,
            )
        )
        copies[-1].start()
    both = halves[chan]
    for step, copy in enumerate(copies):
        copy.wait()
        both += joined[step]
    far_out[...] = both[0:rank].astype(BF16)
    back_out[...] = both[rank : 2 * rank].astype(BF16)


def slot_row(index_ref, count_ref, blocks, block, slot):
    base = lax.axis_index("curve") * blocks - blocks
    row = index_ref[slot, block] - base
    return jnp.where(slot < count_ref[block], row, 2 * blocks)


def chunk_copy(hbm_ref, vmem_ref, sem, chunk):
    rows = pl.ds(chunk * STEP, STEP)
    return pltpu.make_async_copy(hbm_ref.at[rows], vmem_ref.at[rows], sem.at[chunk])


def backward_kernel(index_ref, count_ref, tile_hbm, dy_ref, left_ref, own_ref, tiles, total, sem):
    blocks, slots, panels, _ = tiles.shape
    chunks = blocks // STEP
    for chunk in range(chunks):
        chunk_copy(tile_hbm, tiles, sem, chunk).start()

    @pl.loop(0, 2 * blocks + 1)
    def _(row):
        total[row] = jnp.zeros(total.shape[1:], F32)

    @pl.loop(0, chunks)
    def _(chunk):
        chunk_copy(tile_hbm, tiles, sem, chunk).wait()
        for i in range(STEP):
            block = chunk * STEP + i
            turned = dy_ref[block].T
            for k in range(0, slots, 2):
                pair = jnp.concatenate([tiles[block, k], tiles[block, k + 1]], axis=1)
                term = jnp.dot(turned, pair, preferred_element_type=F32)
                for half in range(2):
                    row = slot_row(index_ref, count_ref, blocks, block, k + half)
                    total[row] += term[:, half * panels : (half + 1) * panels]

    @pl.loop(0, blocks)
    def _(row):
        left_ref[row] = total[row].astype(BF16)
        own_ref[row] = total[blocks + row]


def forward_kernel(
    index_ref, count_ref, tile_hbm, before_hbm, x_hbm, bout_ref, far_ref, out_hbm,
    tiles, held, result, sem, held_sem, out_sem,
):
    blocks, slots, panels, _ = tiles.shape
    chunks = blocks // STEP
    loads = [
        pltpu.make_async_copy(x_hbm, held.at[pl.ds(blocks, blocks)], held_sem.at[0]),
        pltpu.make_async_copy(before_hbm, held.at[pl.ds(0, blocks)], held_sem.at[1]),
    ]
    for load in loads:
        load.start()
    for chunk in range(chunks):
        chunk_copy(tile_hbm, tiles, sem, chunk).start()
    held[2 * blocks] = jnp.zeros(held.shape[1:], BF16)
    for load in loads:
        load.wait()
    far = far_ref[...]

    @pl.loop(0, chunks)
    def _(chunk):
        chunk_copy(tile_hbm, tiles, sem, chunk).wait()
        for i in range(STEP):
            block = chunk * STEP + i
            left = jnp.concatenate([tiles[block, k] for k in range(slots)], axis=1)
            right = jnp.concatenate(
                [held[slot_row(index_ref, count_ref, blocks, block, k)] for k in range(slots)],
                axis=0,
            )
            near = jnp.dot(left, right, preferred_element_type=F32)
            near += lax.dot_general(
                bout_ref[block], far, (((0,), (0,)), ((), ())), preferred_element_type=F32
            )
            result[block] = near.astype(BF16)
        chunk_copy(result, out_hbm, out_sem, chunk).start()

    @pl.loop(0, chunks)
    def _(chunk):
        chunk_copy(result, out_hbm, out_sem, chunk).wait()


def gradient_kernel(own_ref, arrived_ref, bin_ref, back_ref, out_ref):
    back = back_ref[...]
    panels = bin_ref.shape[2]
    row = lax.broadcasted_iota(jnp.int32, (panels, panels), 0)
    col = lax.broadcasted_iota(jnp.int32, (panels, panels), 1)
    eye = jnp.where(row == col, 1.0, 0.0).astype(BF16)
    twice = jnp.concatenate([eye, eye], axis=1)
    for i in range(own_ref.shape[0]):
        turned = own_ref[i] + arrived_ref[i].astype(F32)
        high = turned.astype(BF16)
        low = (turned - high.astype(F32)).astype(BF16)
        grad = lax.dot_general(
            twice,
            jnp.concatenate([high, low], axis=1),
            (((1,), (1,)), ((), ())),
            preferred_element_type=F32,
        )
        grad += lax.dot_general(
            bin_ref[i], back, (((0,), (0,)), ((), ())), preferred_element_type=F32
        )
        out_ref[i] = grad.astype(BF16)


def body(
    features,
    cotangent,
    near_kernel,
    near_index,
    near_count,
    basis_in,
    basis_out,
    far_kernel,
    far_index,
    channel_mix,
):
    blocks, slots, panels, _ = near_kernel.shape
    width = features.shape[1]
    rank = basis_in.shape[1]
    x = features.reshape(blocks, panels, width)
    dy = cotangent.reshape(blocks, panels, width)
    before = shifted(features, "curve", 1).reshape(blocks, panels, width)
    slot_index = near_index.T
    bout_turned = basis_out.transpose(0, 2, 1)
    tile_shape = (panels, width)
    part = blocks // 2
    chunks = blocks // STEP

    def by_step(*shape):
        zeros = (0,) * (len(shape) - 1)
        return pl.BlockSpec(shape, lambda n, *_: (n,) + zeros)

    smem = pl.BlockSpec(memory_space=pltpu.SMEM)
    vmem = pl.BlockSpec(memory_space=pltpu.VMEM)
    anywhere = pl.BlockSpec(memory_space=pl.ANY)
    hbm = pl.BlockSpec(memory_space=pltpu.MemorySpace.HBM)
    groups, shares = lax.axis_size("curve"), lax.axis_size("chan")
    outgoing = pl.pallas_call(
        bundle_kernel,
        out_shape=jax.ShapeDtypeStruct((groups, 2 * rank, width), BF16),
        in_specs=[smem] + [vmem] * 5,
        out_specs=vmem,
        compiler_params=params(60),
        name="bundle",
    )(far_index[0], x, dy, basis_in, bout_turned, far_kernel[0])

    half_flops = 2 * blocks * slots * panels * panels * width
    tile_bytes = 2 * near_kernel.size
    left, own = pl.pallas_call(
        backward_kernel,
        out_shape=(
            jax.ShapeDtypeStruct((blocks, width, panels), BF16),
            jax.ShapeDtypeStruct((blocks, width, panels), F32),
        ),
        in_specs=[smem, smem, hbm, vmem],
        out_specs=(vmem, vmem),
        scratch_shapes=[
            pltpu.VMEM((blocks, slots, panels, panels), BF16),
            pltpu.VMEM((2 * blocks + 1, width, panels), F32),
            pltpu.SemaphoreType.DMA((chunks,)),
        ],
        compiler_params=params(57),
        cost_estimate=pl.CostEstimate(
            flops=4 * half_flops, bytes_accessed=2 * tile_bytes, transcendentals=0
        ),
        name="backward",
    )(slot_index, near_count, near_kernel, dy)

    left, outgoing = lax.optimization_barrier((left, outgoing))
    far_low, back_low = pl.pallas_call(
        functools.partial(exchange_kernel, groups, shares),
        out_shape=(jax.ShapeDtypeStruct((rank, width), BF16),) * 2,
        in_specs=[smem] + [vmem] * 3,
        out_specs=(vmem, vmem),
        scratch_shapes=[
            pltpu.VMEM((groups, 2 * rank, width), BF16),
            pltpu.VMEM((shares, 2 * rank, width), F32),
            pltpu.VMEM((max(1, shares - 1), 2 * rank, width), F32),
            pltpu.SemaphoreType.DMA((groups,)),
            pltpu.SemaphoreType.DMA((groups,)),
            pltpu.SemaphoreType.DMA((shares,)),
            pltpu.SemaphoreType.DMA((shares,)),
        ],
        compiler_params=pltpu.CompilerParams(
            collective_id=0, has_side_effects=True, vmem_limit_bytes=40 * 1024 * 1024
        ),
        name="exchange",
    )(far_index[0], outgoing, far_kernel[0], channel_mix)
    left, far_low = lax.optimization_barrier((left, far_low))
    arrived = shifted(left, "curve", -1)

    layer = pl.pallas_call(
        forward_kernel,
        out_shape=jax.ShapeDtypeStruct((blocks, panels, width), BF16),
        in_specs=[smem, smem, hbm, anywhere, anywhere, vmem, vmem],
        out_specs=hbm,
        scratch_shapes=[
            pltpu.VMEM((blocks, slots, panels, panels), BF16),
            pltpu.VMEM((2 * blocks + 1, panels, width), BF16),
            pltpu.VMEM((blocks, panels, width), BF16),
            pltpu.SemaphoreType.DMA((chunks,)),
            pltpu.SemaphoreType.DMA((2,)),
            pltpu.SemaphoreType.DMA((chunks,)),
        ],
        compiler_params=params(40),
        cost_estimate=pl.CostEstimate(
            flops=4 * half_flops, bytes_accessed=2 * tile_bytes, transcendentals=0
        ),
        name="forward",
    )(slot_index, near_count, near_kernel, before, x, bout_turned, far_low)

    grad = pl.pallas_call(
        gradient_kernel,
        out_shape=jax.ShapeDtypeStruct((blocks, panels, width), BF16),
        grid=(2,),
        in_specs=[
            by_step(part, width, panels),
            by_step(part, width, panels),
            by_step(part, rank, panels),
            cover((rank, width)),
        ],
        out_specs=by_step(part, *tile_shape),
        compiler_params=params(40),
        name="gradient",
    )(own, arrived, basis_in, back_low)
    return (layer.reshape(blocks * panels, width), grad.reshape(blocks * panels, width))


def solution(mesh):
    return jax.shard_map(
        body,
        mesh=mesh,
        in_specs=(
            P("curve", "chan"),
            P("curve", "chan"),
            P("curve", None, None, None),
            P("curve", None),
            P("curve"),
            P("curve", None, None),
            P("curve", None, None),
            P("curve", None, None, None),
            P("curve", None),
            P(),
        ),
        out_specs=(P("curve", "chan"), P("curve", "chan")),
        check_vma=False,
    )
```

```python
import functools

import jax
import jax.numpy as jnp
from jax import lax
from jax.experimental import pallas as pl
from jax.experimental.pallas import tpu as pltpu
from jax.sharding import PartitionSpec as P

F32 = jnp.float32
BF16 = jnp.bfloat16
EXACT = lax.Precision.HIGHEST
STEP = 4


def shifted(value, axis, steps):
    count = lax.axis_size(axis)
    leading, last = (max(0, -steps), min(count, count - steps))
    return lax.ppermute(value, axis, [(source, source + steps) for source in range(leading, last)])


def cover(shape):
    zeros = (0,) * len(shape)
    return pl.BlockSpec(shape, lambda *_: zeros)


def params(mib=60):
    return pltpu.CompilerParams(vmem_limit_bytes=mib * 1024 * 1024)


def bundle_kernel(part_ref, x_ref, dy_ref, bin_ref, bout_ref, far_ref, out_ref):
    blocks, rank, width = bin_ref.shape[0], bin_ref.shape[1], x_ref.shape[2]
    partners = far_ref.shape[0]
    coarse = jnp.zeros((rank, width), F32)
    dfar = jnp.zeros((rank, width), F32)
    for b in range(blocks):
        coarse += jnp.dot(bin_ref[b], x_ref[b], preferred_element_type=F32)
        dfar += jnp.dot(bout_ref[b], dy_ref[b], preferred_element_type=F32)
    coarse = coarse.astype(BF16)
    spread = [
        lax.dot_general(
            far_ref[a], dfar, (((0,), (0,)), ((), ())), precision=EXACT, preferred_element_type=F32
        )
        for a in range(partners)
    ]

    @pl.loop(0, out_ref.shape[0])
    def _(group):
        share = jnp.zeros((rank, width), F32)
        for a in range(partners):
            share += jnp.where(part_ref[a] == group, 1.0, 0.0) * spread[a]
        out_ref[group, 0:rank] = coarse
        out_ref[group, rank : 2 * rank] = share.astype(BF16)


def exchange_kernel(
    groups, shares, part_ref, send_ref, far_ref, mix_ref, far_out, back_out,
    held, halves, joined, turned, send_sem, recv_sem, send_half, recv_half,
):
    me, chan = lax.axis_index("curve"), lax.axis_index("chan")
    rank, width = far_out.shape
    partners = far_ref.shape[0]
    barrier = pltpu.get_barrier_semaphore()

    @pl.loop(1, groups)
    def _(step):
        pl.semaphore_signal(
            barrier,
            inc=1,
            device_id=(lax.rem(me + step, groups), chan),
            device_id_type=pl.DeviceIdType.MESH,
        )

    for step in range(1, shares):
        pl.semaphore_signal(
            barrier,
            inc=1,
            device_id=(me, lax.rem(chan + step, shares)),
            device_id_type=pl.DeviceIdType.MESH,
        )
    pl.semaphore_wait(barrier, groups + shares - 2)

    def along_curve(step):
        other = lax.rem(me + step, groups)
        return pltpu.make_async_remote_copy(
            src_ref=send_ref.at[other],
            dst_ref=held.at[me],
            send_sem=send_sem.at[step],
            recv_sem=recv_sem.at[step],
            device_id=(other, chan),
            device_id_type=pl.DeviceIdType.MESH,
        )

    @pl.loop(1, groups)
    def _(step):
        along_curve(step).start()

    held[me] = send_ref[me]
    own = pl.ds(pl.multiple_of(chan * width, width), width)
    far = jnp.concatenate([far_ref[a] for a in range(partners)], axis=1)
    high = far.astype(BF16)
    low = (far - high.astype(F32)).astype(BF16)
    turned[...] = mix_ref[:, own].T

    @pl.loop(1, groups)
    def _(step):
        along_curve(step).wait()

    rows = jnp.concatenate([held[part_ref[a], 0:rank] for a in range(partners)], axis=0)
    coef = jnp.dot(high, rows, preferred_element_type=F32)
    coef += jnp.dot(low, rows, preferred_element_type=F32)
    total = lax.fori_loop(
        0,
        groups,
        lambda g, acc: acc + held[g, rank : 2 * rank].astype(F32),
        jnp.zeros((rank, width), F32),
    )
    term = jnp.dot(coef, mix_ref[own, :], precision=EXACT, preferred_element_type=F32)
    back = jnp.dot(total, turned[...], precision=EXACT, preferred_element_type=F32)
    for s in range(shares):
        halves[s, 0:rank] = term[:, s * width : (s + 1) * width]
        halves[s, rank : 2 * rank] = back[:, s * width : (s + 1) * width]

    copies = []
    for step in range(1, shares):
        other = lax.rem(chan + step, shares)
        copies.append(
            pltpu.make_async_remote_copy(
                src_ref=halves.at[other],
                dst_ref=joined.at[step - 1],
                send_sem=send_half.at[step],
                recv_sem=recv_half.at[step],
                device_id=(me, other),
                device_id_type=pl.DeviceIdType.MESH,
            )
        )
        copies[-1].start()
    both = halves[chan]
    for step, copy in enumerate(copies):
        copy.wait()
        both += joined[step]
    far_out[...] = both[0:rank].astype(BF16)
    back_out[...] = both[rank : 2 * rank].astype(BF16)


def slot_row(index_ref, count_ref, blocks, block, slot):
    base = lax.axis_index("curve") * blocks - blocks
    row = index_ref[slot, block] - base
    return jnp.where(slot < count_ref[block], row, 2 * blocks)


def chunk_copy(hbm_ref, vmem_ref, sem, chunk):
    rows = pl.ds(chunk * STEP, STEP)
    return pltpu.make_async_copy(hbm_ref.at[rows], vmem_ref.at[rows], sem.at[chunk])


def backward_kernel(index_ref, count_ref, tile_hbm, dy_ref, left_ref, own_ref, tiles, total, sem):
    blocks, slots, panels, _ = tiles.shape
    chunks = blocks // STEP
    for chunk in range(chunks):
        chunk_copy(tile_hbm, tiles, sem, chunk).start()

    @pl.loop(0, 2 * blocks + 1)
    def _(row):
        total[row] = jnp.zeros(total.shape[1:], F32)

    @pl.loop(0, chunks)
    def _(chunk):
        chunk_copy(tile_hbm, tiles, sem, chunk).wait()
        for i in range(STEP):
            block = chunk * STEP + i
            turned = dy_ref[block].T
            for k in range(0, slots, 2):
                pair = jnp.concatenate([tiles[block, k], tiles[block, k + 1]], axis=1)
                term = jnp.dot(turned, pair, preferred_element_type=F32)
                for half in range(2):
                    row = slot_row(index_ref, count_ref, blocks, block, k + half)
                    total[row] += term[:, half * panels : (half + 1) * panels]

    @pl.loop(0, blocks)
    def _(row):
        left_ref[row] = total[row].astype(BF16)
        own_ref[row] = total[blocks + row]


def forward_kernel(
    index_ref, count_ref, tile_hbm, before_hbm, x_hbm, bout_ref, far_ref, out_hbm,
    tiles, held, result, sem, held_sem, out_sem,
):
    blocks, slots, panels, _ = tiles.shape
    chunks = blocks // STEP
    loads = [
        pltpu.make_async_copy(x_hbm, held.at[pl.ds(blocks, blocks)], held_sem.at[0]),
        pltpu.make_async_copy(before_hbm, held.at[pl.ds(0, blocks)], held_sem.at[1]),
    ]
    for load in loads:
        load.start()
    for chunk in range(chunks):
        chunk_copy(tile_hbm, tiles, sem, chunk).start()
    held[2 * blocks] = jnp.zeros(held.shape[1:], BF16)
    for load in loads:
        load.wait()
    far = far_ref[...]

    @pl.loop(0, chunks)
    def _(chunk):
        chunk_copy(tile_hbm, tiles, sem, chunk).wait()
        for i in range(STEP):
            block = chunk * STEP + i
            left = jnp.concatenate([tiles[block, k] for k in range(slots)], axis=1)
            right = jnp.concatenate(
                [held[slot_row(index_ref, count_ref, blocks, block, k)] for k in range(slots)],
                axis=0,
            )
            near = jnp.dot(left, right, preferred_element_type=F32)
            near += lax.dot_general(
                bout_ref[block], far, (((0,), (0,)), ((), ())), preferred_element_type=F32
            )
            result[block] = near.astype(BF16)
        chunk_copy(result, out_hbm, out_sem, chunk).start()

    @pl.loop(0, chunks)
    def _(chunk):
        chunk_copy(result, out_hbm, out_sem, chunk).wait()


def gradient_kernel(own_ref, arrived_ref, bin_ref, back_ref, out_ref):
    back = back_ref[...]
    panels = bin_ref.shape[2]
    row = lax.broadcasted_iota(jnp.int32, (panels, panels), 0)
    col = lax.broadcasted_iota(jnp.int32, (panels, panels), 1)
    eye = jnp.where(row == col, 1.0, 0.0).astype(BF16)
    twice = jnp.concatenate([eye, eye], axis=1)
    for i in range(own_ref.shape[0]):
        turned = own_ref[i] + arrived_ref[i].astype(F32)
        high = turned.astype(BF16)
        low = (turned - high.astype(F32)).astype(BF16)
        grad = lax.dot_general(
            twice,
            jnp.concatenate([high, low], axis=1),
            (((1,), (1,)), ((), ())),
            preferred_element_type=F32,
        )
        grad += lax.dot_general(
            bin_ref[i], back, (((0,), (0,)), ((), ())), preferred_element_type=F32
        )
        out_ref[i] = grad.astype(BF16)


def body(
    features,
    cotangent,
    near_kernel,
    near_index,
    near_count,
    basis_in,
    basis_out,
    far_kernel,
    far_index,
    channel_mix,
):
    blocks, slots, panels, _ = near_kernel.shape
    width = features.shape[1]
    rank = basis_in.shape[1]
    x = features.reshape(blocks, panels, width)
    dy = cotangent.reshape(blocks, panels, width)
    before = shifted(features, "curve", 1).reshape(blocks, panels, width)
    slot_index = near_index.T
    bout_turned = basis_out.transpose(0, 2, 1)
    tile_shape = (panels, width)
    part = blocks // 2
    chunks = blocks // STEP

    def by_step(*shape):
        zeros = (0,) * (len(shape) - 1)
        return pl.BlockSpec(shape, lambda n, *_: (n,) + zeros)

    smem = pl.BlockSpec(memory_space=pltpu.SMEM)
    vmem = pl.BlockSpec(memory_space=pltpu.VMEM)
    anywhere = pl.BlockSpec(memory_space=pl.ANY)
    hbm = pl.BlockSpec(memory_space=pltpu.MemorySpace.HBM)
    groups, shares = lax.axis_size("curve"), lax.axis_size("chan")
    outgoing = pl.pallas_call(
        bundle_kernel,
        out_shape=jax.ShapeDtypeStruct((groups, 2 * rank, width), BF16),
        in_specs=[smem] + [vmem] * 5,
        out_specs=vmem,
        compiler_params=params(60),
        name="bundle",
    )(far_index[0], x, dy, basis_in, bout_turned, far_kernel[0])

    half_flops = 2 * blocks * slots * panels * panels * width
    tile_bytes = 2 * near_kernel.size
    left, own = pl.pallas_call(
        backward_kernel,
        out_shape=(
            jax.ShapeDtypeStruct((blocks, width, panels), BF16),
            jax.ShapeDtypeStruct((blocks, width, panels), F32),
        ),
        in_specs=[smem, smem, hbm, vmem],
        out_specs=(vmem, vmem),
        scratch_shapes=[
            pltpu.VMEM((blocks, slots, panels, panels), BF16),
            pltpu.VMEM((2 * blocks + 1, width, panels), F32),
            pltpu.SemaphoreType.DMA((chunks,)),
        ],
        compiler_params=params(57),
        cost_estimate=pl.CostEstimate(
            flops=4 * half_flops, bytes_accessed=2 * tile_bytes, transcendentals=0
        ),
        name="backward",
    )(slot_index, near_count, near_kernel, dy)

    left, outgoing = lax.optimization_barrier((left, outgoing))
    far_low, back_low = pl.pallas_call(
        functools.partial(exchange_kernel, groups, shares),
        out_shape=(jax.ShapeDtypeStruct((rank, width), BF16),) * 2,
        in_specs=[smem] + [vmem] * 3,
        out_specs=(vmem, vmem),
        scratch_shapes=[
            pltpu.VMEM((groups, 2 * rank, width), BF16),
            pltpu.VMEM((shares, 2 * rank, width), F32),
            pltpu.VMEM((max(1, shares - 1), 2 * rank, width), F32),
            pltpu.VMEM((width, shares * width), F32),
            pltpu.SemaphoreType.DMA((groups,)),
            pltpu.SemaphoreType.DMA((groups,)),
            pltpu.SemaphoreType.DMA((shares,)),
            pltpu.SemaphoreType.DMA((shares,)),
        ],
        compiler_params=pltpu.CompilerParams(
            collective_id=0, has_side_effects=True, vmem_limit_bytes=40 * 1024 * 1024
        ),
        cost_estimate=pl.CostEstimate(
            flops=0, bytes_accessed=4 * tile_bytes, transcendentals=0
        ),
        name="exchange",
    )(far_index[0], outgoing, far_kernel[0], channel_mix)
    left, back_low = lax.optimization_barrier((left, back_low))
    arrived = shifted(left, "curve", -1)

    layer = pl.pallas_call(
        forward_kernel,
        out_shape=jax.ShapeDtypeStruct((blocks, panels, width), BF16),
        in_specs=[smem, smem, hbm, anywhere, anywhere, vmem, vmem],
        out_specs=hbm,
        scratch_shapes=[
            pltpu.VMEM((blocks, slots, panels, panels), BF16),
            pltpu.VMEM((2 * blocks + 1, panels, width), BF16),
            pltpu.VMEM((blocks, panels, width), BF16),
            pltpu.SemaphoreType.DMA((chunks,)),
            pltpu.SemaphoreType.DMA((2,)),
            pltpu.SemaphoreType.DMA((chunks,)),
        ],
        compiler_params=params(57),
        cost_estimate=pl.CostEstimate(
            flops=4 * half_flops, bytes_accessed=2 * tile_bytes, transcendentals=0
        ),
        name="forward",
    )(slot_index, near_count, near_kernel, before, x, bout_turned, far_low)

    grad = pl.pallas_call(
        gradient_kernel,
        out_shape=jax.ShapeDtypeStruct((blocks, panels, width), BF16),
        grid=(2,),
        in_specs=[
            by_step(part, width, panels),
            by_step(part, width, panels),
            by_step(part, rank, panels),
            cover((rank, width)),
        ],
        out_specs=by_step(part, *tile_shape),
        compiler_params=params(40),
        name="gradient",
    )(own, arrived, basis_in, back_low)
    return (layer.reshape(blocks * panels, width), grad.reshape(blocks * panels, width))


def solution(mesh):
    return jax.shard_map(
        body,
        mesh=mesh,
        in_specs=(
            P("curve", "chan"),
            P("curve", "chan"),
            P("curve", None, None, None),
            P("curve", None),
            P("curve"),
            P("curve", None, None),
            P("curve", None, None),
            P("curve", None, None, None),
            P("curve", None),
            P(),
        ),
        out_specs=(P("curve", "chan"), P("curve", "chan")),
        check_vma=False,
    )
```

```python
import functools

import jax
import jax.numpy as jnp
from jax import lax
from jax.experimental import pallas as pl
from jax.experimental.pallas import tpu as pltpu
from jax.sharding import PartitionSpec as P

F32 = jnp.float32
BF16 = jnp.bfloat16
EXACT = lax.Precision.HIGHEST
STEP = 4


def shifted(value, axis, steps):
    count = lax.axis_size(axis)
    leading, last = (max(0, -steps), min(count, count - steps))
    return lax.ppermute(value, axis, [(source, source + steps) for source in range(leading, last)])


def cover(shape):
    zeros = (0,) * len(shape)
    return pl.BlockSpec(shape, lambda *_: zeros)


def params(mib=60):
    return pltpu.CompilerParams(vmem_limit_bytes=mib * 1024 * 1024)


def bundle_kernel(part_ref, x_ref, dy_ref, bin_ref, bout_ref, far_ref, out_ref):
    blocks, rank, width = bin_ref.shape[0], bin_ref.shape[1], x_ref.shape[2]
    partners = far_ref.shape[0]
    coarse = jnp.zeros((rank, width), F32)
    dfar = jnp.zeros((rank, width), F32)
    for b in range(blocks):
        coarse += jnp.dot(bin_ref[b], x_ref[b], preferred_element_type=F32)
        dfar += jnp.dot(bout_ref[b], dy_ref[b], preferred_element_type=F32)
    coarse = coarse.astype(BF16)
    spread = [
        lax.dot_general(
            far_ref[a], dfar, (((0,), (0,)), ((), ())), precision=EXACT, preferred_element_type=F32
        )
        for a in range(partners)
    ]

    @pl.loop(0, out_ref.shape[0])
    def _(group):
        share = jnp.zeros((rank, width), F32)
        for a in range(partners):
            share += jnp.where(part_ref[a] == group, 1.0, 0.0) * spread[a]
        out_ref[group, 0:rank] = coarse
        out_ref[group, rank : 2 * rank] = share.astype(BF16)


def exchange_kernel(
    groups, shares, part_ref, send_ref, far_ref, mix_ref, far_out, back_out,
    held, halves, joined, turned, send_sem, recv_sem, send_half, recv_half,
):
    me, chan = lax.axis_index("curve"), lax.axis_index("chan")
    rank, width = far_out.shape
    partners = far_ref.shape[0]
    barrier = pltpu.get_barrier_semaphore()

    @pl.loop(1, groups)
    def _(step):
        pl.semaphore_signal(
            barrier,
            inc=1,
            device_id=(lax.rem(me + step, groups), chan),
            device_id_type=pl.DeviceIdType.MESH,
        )

    for step in range(1, shares):
        pl.semaphore_signal(
            barrier,
            inc=1,
            device_id=(me, lax.rem(chan + step, shares)),
            device_id_type=pl.DeviceIdType.MESH,
        )
    pl.semaphore_wait(barrier, groups + shares - 2)

    def along_curve(step):
        other = lax.rem(me + step, groups)
        return pltpu.make_async_remote_copy(
            src_ref=send_ref.at[other],
            dst_ref=held.at[me],
            send_sem=send_sem.at[step],
            recv_sem=recv_sem.at[step],
            device_id=(other, chan),
            device_id_type=pl.DeviceIdType.MESH,
        )

    @pl.loop(1, groups)
    def _(step):
        along_curve(step).start()

    held[me] = send_ref[me]
    own = pl.ds(pl.multiple_of(chan * width, width), width)
    far = jnp.concatenate([far_ref[a] for a in range(partners)], axis=1)
    high = far.astype(BF16)
    low = (far - high.astype(F32)).astype(BF16)
    turned[...] = mix_ref[:, own].T

    @pl.loop(1, groups)
    def _(step):
        along_curve(step).wait()

    rows = jnp.concatenate([held[part_ref[a], 0:rank] for a in range(partners)], axis=0)
    coef = jnp.dot(high, rows, preferred_element_type=F32)
    coef += jnp.dot(low, rows, preferred_element_type=F32)
    total = lax.fori_loop(
        0,
        groups,
        lambda g, acc: acc + held[g, rank : 2 * rank].astype(F32),
        jnp.zeros((rank, width), F32),
    )
    term = jnp.dot(coef, mix_ref[own, :], precision=EXACT, preferred_element_type=F32)
    back = jnp.dot(total, turned[...], precision=EXACT, preferred_element_type=F32)
    for s in range(shares):
        halves[s, 0:rank] = term[:, s * width : (s + 1) * width]
        halves[s, rank : 2 * rank] = back[:, s * width : (s + 1) * width]

    copies = []
    for step in range(1, shares):
        other = lax.rem(chan + step, shares)
        copies.append(
            pltpu.make_async_remote_copy(
                src_ref=halves.at[other],
                dst_ref=joined.at[step - 1],
                send_sem=send_half.at[step],
                recv_sem=recv_half.at[step],
                device_id=(me, other),
                device_id_type=pl.DeviceIdType.MESH,
            )
        )
        copies[-1].start()
    both = halves[chan]
    for step, copy in enumerate(copies):
        copy.wait()
        both += joined[step]
    far_out[...] = both[0:rank].astype(BF16)
    back_out[...] = both[rank : 2 * rank].astype(BF16)


def slot_row(index_ref, count_ref, blocks, block, slot):
    base = lax.axis_index("curve") * blocks - blocks
    row = index_ref[slot, block] - base
    return jnp.where(slot < count_ref[block], row, 2 * blocks)


def chunk_copy(hbm_ref, vmem_ref, sem, chunk):
    rows = pl.ds(chunk * STEP, STEP)
    return pltpu.make_async_copy(hbm_ref.at[rows], vmem_ref.at[rows], sem.at[chunk])


def backward_kernel(index_ref, count_ref, tile_hbm, dy_ref, left_ref, own_ref, tiles, total, sem):
    blocks, slots, panels, _ = tiles.shape
    chunks = blocks // STEP
    for chunk in range(chunks):
        chunk_copy(tile_hbm, tiles, sem, chunk).start()

    @pl.loop(0, 2 * blocks + 1)
    def _(row):
        total[row] = jnp.zeros(total.shape[1:], F32)

    @pl.loop(0, chunks)
    def _(chunk):
        chunk_copy(tile_hbm, tiles, sem, chunk).wait()
        for i in range(STEP):
            block = chunk * STEP + i
            turned = dy_ref[block].T
            for k in range(0, slots, 2):
                pair = jnp.concatenate([tiles[block, k], tiles[block, k + 1]], axis=1)
                term = jnp.dot(turned, pair, preferred_element_type=F32)
                for half in range(2):
                    row = slot_row(index_ref, count_ref, blocks, block, k + half)
                    total[row] += term[:, half * panels : (half + 1) * panels]

    @pl.loop(0, blocks)
    def _(row):
        left_ref[row] = total[row].astype(BF16)
        own_ref[row] = total[blocks + row]


def forward_kernel(
    index_ref, count_ref, tile_hbm, before_hbm, x_hbm, bout_ref, far_ref, out_hbm,
    tiles, held, result, sem, held_sem, out_sem,
):
    blocks, slots, panels, _ = tiles.shape
    chunks = blocks // STEP
    loads = [
        pltpu.make_async_copy(x_hbm, held.at[pl.ds(blocks, blocks)], held_sem.at[0]),
        pltpu.make_async_copy(before_hbm, held.at[pl.ds(0, blocks)], held_sem.at[1]),
    ]
    for load in loads:
        load.start()
    for chunk in range(chunks):
        chunk_copy(tile_hbm, tiles, sem, chunk).start()
    held[2 * blocks] = jnp.zeros(held.shape[1:], BF16)
    for load in loads:
        load.wait()
    far = far_ref[...]

    @pl.loop(0, chunks)
    def _(chunk):
        chunk_copy(tile_hbm, tiles, sem, chunk).wait()
        for i in range(STEP):
            block = chunk * STEP + i
            left = jnp.concatenate([tiles[block, k] for k in range(slots)], axis=1)
            right = jnp.concatenate(
                [held[slot_row(index_ref, count_ref, blocks, block, k)] for k in range(slots)],
                axis=0,
            )
            near = jnp.dot(left, right, preferred_element_type=F32)
            near += lax.dot_general(
                bout_ref[block], far, (((0,), (0,)), ((), ())), preferred_element_type=F32
            )
            result[block] = near.astype(BF16)
        chunk_copy(result, out_hbm, out_sem, chunk).start()

    @pl.loop(0, chunks)
    def _(chunk):
        chunk_copy(result, out_hbm, out_sem, chunk).wait()


def gradient_kernel(own_ref, arrived_ref, bin_ref, back_ref, out_ref):
    back = back_ref[...]
    panels = bin_ref.shape[2]
    row = lax.broadcasted_iota(jnp.int32, (panels, panels), 0)
    col = lax.broadcasted_iota(jnp.int32, (panels, panels), 1)
    eye = jnp.where(row == col, 1.0, 0.0).astype(BF16)
    twice = jnp.concatenate([eye, eye], axis=1)
    for i in range(own_ref.shape[0]):
        turned = own_ref[i] + arrived_ref[i].astype(F32)
        high = turned.astype(BF16)
        low = (turned - high.astype(F32)).astype(BF16)
        grad = lax.dot_general(
            twice,
            jnp.concatenate([high, low], axis=1),
            (((1,), (1,)), ((), ())),
            preferred_element_type=F32,
        )
        grad += lax.dot_general(
            bin_ref[i], back, (((0,), (0,)), ((), ())), preferred_element_type=F32
        )
        out_ref[i] = grad.astype(BF16)


def body(
    features,
    cotangent,
    near_kernel,
    near_index,
    near_count,
    basis_in,
    basis_out,
    far_kernel,
    far_index,
    channel_mix,
):
    blocks, slots, panels, _ = near_kernel.shape
    width = features.shape[1]
    rank = basis_in.shape[1]
    x = features.reshape(blocks, panels, width)
    dy = cotangent.reshape(blocks, panels, width)
    before = shifted(features, "curve", 1).reshape(blocks, panels, width)
    slot_index = near_index.T
    bout_turned = basis_out.transpose(0, 2, 1)
    tile_shape = (panels, width)
    part = blocks // 2
    chunks = blocks // STEP

    def by_step(*shape):
        zeros = (0,) * (len(shape) - 1)
        return pl.BlockSpec(shape, lambda n, *_: (n,) + zeros)

    smem = pl.BlockSpec(memory_space=pltpu.SMEM)
    vmem = pl.BlockSpec(memory_space=pltpu.VMEM)
    anywhere = pl.BlockSpec(memory_space=pl.ANY)
    hbm = pl.BlockSpec(memory_space=pltpu.MemorySpace.HBM)
    groups, shares = lax.axis_size("curve"), lax.axis_size("chan")
    outgoing = pl.pallas_call(
        bundle_kernel,
        out_shape=jax.ShapeDtypeStruct((groups, 2 * rank, width), BF16),
        in_specs=[smem] + [vmem] * 5,
        out_specs=vmem,
        compiler_params=params(60),
        name="bundle",
    )(far_index[0], x, dy, basis_in, bout_turned, far_kernel[0])

    half_flops = 2 * blocks * slots * panels * panels * width
    tile_bytes = 2 * near_kernel.size
    left, own = pl.pallas_call(
        backward_kernel,
        out_shape=(
            jax.ShapeDtypeStruct((blocks, width, panels), BF16),
            jax.ShapeDtypeStruct((blocks, width, panels), F32),
        ),
        in_specs=[smem, smem, hbm, vmem],
        out_specs=(vmem, vmem),
        scratch_shapes=[
            pltpu.VMEM((blocks, slots, panels, panels), BF16),
            pltpu.VMEM((2 * blocks + 1, width, panels), F32),
            pltpu.SemaphoreType.DMA((chunks,)),
        ],
        compiler_params=params(57),
        cost_estimate=pl.CostEstimate(
            flops=4 * half_flops, bytes_accessed=2 * tile_bytes, transcendentals=0
        ),
        name="backward",
    )(slot_index, near_count, near_kernel, dy)

    left, outgoing = lax.optimization_barrier((left, outgoing))
    far_low, back_low = pl.pallas_call(
        functools.partial(exchange_kernel, groups, shares),
        out_shape=(jax.ShapeDtypeStruct((rank, width), BF16),) * 2,
        in_specs=[smem] + [vmem] * 3,
        out_specs=(vmem, vmem),
        scratch_shapes=[
            pltpu.VMEM((groups, 2 * rank, width), BF16),
            pltpu.VMEM((shares, 2 * rank, width), F32),
            pltpu.VMEM((max(1, shares - 1), 2 * rank, width), F32),
            pltpu.VMEM((width, shares * width), F32),
            pltpu.SemaphoreType.DMA((groups,)),
            pltpu.SemaphoreType.DMA((groups,)),
            pltpu.SemaphoreType.DMA((shares,)),
            pltpu.SemaphoreType.DMA((shares,)),
        ],
        compiler_params=pltpu.CompilerParams(
            collective_id=0, has_side_effects=True, vmem_limit_bytes=40 * 1024 * 1024
        ),
        cost_estimate=pl.CostEstimate(
            flops=0, bytes_accessed=4 * tile_bytes, transcendentals=0
        ),
        name="exchange",
    )(far_index[0], outgoing, far_kernel[0], channel_mix)
    arrived = shifted(left, "curve", -1)

    layer = pl.pallas_call(
        forward_kernel,
        out_shape=jax.ShapeDtypeStruct((blocks, panels, width), BF16),
        in_specs=[smem, smem, hbm, anywhere, anywhere, vmem, vmem],
        out_specs=hbm,
        scratch_shapes=[
            pltpu.VMEM((blocks, slots, panels, panels), BF16),
            pltpu.VMEM((2 * blocks + 1, panels, width), BF16),
            pltpu.VMEM((blocks, panels, width), BF16),
            pltpu.SemaphoreType.DMA((chunks,)),
            pltpu.SemaphoreType.DMA((2,)),
            pltpu.SemaphoreType.DMA((chunks,)),
        ],
        compiler_params=params(57),
        cost_estimate=pl.CostEstimate(
            flops=4 * half_flops, bytes_accessed=2 * tile_bytes, transcendentals=0
        ),
        name="forward",
    )(slot_index, near_count, near_kernel, before, x, bout_turned, far_low)

    grad = pl.pallas_call(
        gradient_kernel,
        out_shape=jax.ShapeDtypeStruct((blocks, panels, width), BF16),
        grid=(2,),
        in_specs=[
            by_step(part, width, panels),
            by_step(part, width, panels),
            by_step(part, rank, panels),
            cover((rank, width)),
        ],
        out_specs=by_step(part, *tile_shape),
        compiler_params=params(40),
        name="gradient",
    )(own, arrived, basis_in, back_low)
    return (layer.reshape(blocks * panels, width), grad.reshape(blocks * panels, width))


def solution(mesh):
    return jax.shard_map(
        body,
        mesh=mesh,
        in_specs=(
            P("curve", "chan"),
            P("curve", "chan"),
            P("curve", None, None, None),
            P("curve", None),
            P("curve"),
            P("curve", None, None),
            P("curve", None, None),
            P("curve", None, None, None),
            P("curve", None),
            P(),
        ),
        out_specs=(P("curve", "chan"), P("curve", "chan")),
        check_vma=False,
    )
```
